256 devices in a mesh: cells: 64 (over z, x, core), cls: 4 (over y).
Axes of the slice: x: 4, y: 4, z: 8, core: 2. Of those that a mesh axis runs over, the one named last changes fastest.
Arguments:
- cotangent: float32 [4, 8192, 24, 128], P('cls', 'cells'), may hold values from -6 to 6
- departure: int32 [2, 8192], replicated, may hold values from 0 to 8191, as said below
- interp: bfloat16 [2, 8192, 128, 128], P(None, ('cells', 'cls')), may hold values from -0.5 to 0.5
- vertical_inv: float32 [4, 4, 24, 24], replicated, may hold values from -0.35 to 1.2
- regime: int32 [8192, 128], P('cells'), may hold values from 0 to 3
- bed_rate: float32 [4], replicated, may hold values from 0.3 to 1.5
Outputs:
- initial_grad: float32 [4, 8192, 24, 128], P('cls', 'cells')
The draws below stay inside these ranges and needn't reach their ends.
Inputs may be any that keep to these rules, and one draw needn't show every extreme that they name: For a block of partition p (blocks p * 128 to p * 128 + 127), departure lies in partition p - d with 0 <= d <= min(4, p); in each step at most 32 blocks of one partition depart from one other partition; both bounds are reached.
All inputs are finite; a program needn't handle non-finite values.
Results may differ from the reference program's by a relative error of at most 0.0036.
Values may be sent and summed in bfloat16 or wider, within the bound.
A program may use at most 64 MiB of HBM per device.

```python
import math
import jax
import jax.numpy as jnp
from jax import lax

ROWS = 128
LAYERS = 24
NSET = 4
REACH = 4
STEPS = 2
BLK_DEV = 128
CAP = 32
CLASSES = 4
NBLK = 8192
N_CELLS = 64


def draw_departure(key, part):
    base = jax.random.fold_in(key, 11)
    first_key, second_key = jax.random.split(base)
    owner = jnp.broadcast_to((jnp.arange(NBLK, dtype=jnp.int32) // BLK_DEV)[None, :], (STEPS, NBLK))
    offset = jax.random.randint(first_key, (STEPS, NBLK), 0, REACH + 1).astype(jnp.int32)
    offset = jnp.minimum(offset, owner)
    leading = (jnp.arange(NBLK, dtype=jnp.int32) % BLK_DEV == 0)[None, :] & (owner >= REACH)
    offset = jnp.where(leading, REACH, offset)
    grouped = offset.reshape(STEPS, N_CELLS, BLK_DEV)
    one_hot = (grouped[..., None] == jnp.arange(REACH + 1, dtype=jnp.int32)).astype(jnp.int32)
    ranking = jnp.sum((jnp.cumsum(one_hot, axis=2) - 1) * one_hot, axis=3).reshape(STEPS, NBLK)
    offset = jnp.where((offset > 0) & (ranking >= CAP), 0, offset)
    target = jax.random.randint(second_key, (STEPS, NBLK), 0, BLK_DEV).astype(jnp.int32)
    return ((owner - offset) * BLK_DEV + target).astype(jnp.int32)


def draw_vertical_inv(key, part):
    base = jax.random.fold_in(key, 7)
    first_key, second_key = jax.random.split(base)
    shape = (CLASSES, NSET, LAYERS, LAYERS)
    levels = jnp.arange(LAYERS)
    distance = jnp.abs(levels[:, None] - levels[None, :]).astype(jnp.float32)
    decay = jnp.power(jnp.float32(0.35), distance)
    offdiag = jax.random.uniform(first_key, shape, jnp.float32, -1.0, 1.0) * decay
    diagonal = jax.random.uniform(second_key, shape, jnp.float32, 0.8, 1.2)
    return jnp.where(distance == 0.0, diagonal, offdiag).astype(jnp.float32)


def touch_ends(drawn, stream_key, low, high):
    index_at = [jax.random.randint(jax.random.fold_in(stream_key, axis), (), 0, length) for axis, length in enumerate(drawn.shape)]
    main_axis = drawn.shape.index(max(drawn.shape))
    next_to = index_at[:main_axis] + [(index_at[main_axis] + 1) % drawn.shape[main_axis]] + index_at[main_axis + 1:]
    return drawn.at[tuple(index_at)].set(low).at[tuple(next_to)].set(high)


def block_scale(own_key, shape, pieces, smallest, high):
    loudness = 1.0
    for axis_at, blocks in pieces:
        draws = jax.random.uniform(jax.random.fold_in(jax.random.fold_in(own_key, 6), axis_at), (blocks,), jnp.float32, smallest / len(pieces), high / len(pieces))
        loudness = loudness * jnp.repeat(jnp.exp(draws), shape[axis_at] // blocks).reshape((-1,) + (1,) * (len(shape) - 1 - axis_at))
    return loudness


def bell_draw(stream_key, extent, scale, bound, cuts=(), kind=jnp.bfloat16):
    drawn = jax.random.normal(stream_key, extent, jnp.float32) * scale
    if len(cuts) > 0:
        drawn = block_scale(stream_key, extent, cuts, -0.22, 0.18) * drawn
    return jnp.clip(drawn, min=-bound, max=bound).astype(kind)


def setup_inputs(seed: int = 0) -> dict:
    seeds = jax.random.split(jax.random.key(seed), 7)
    cotangent = bell_draw(seeds[0], (CLASSES, NBLK, LAYERS, ROWS), 1.0, 6.0, ((0, 4), (1, 64)), jnp.float32)
    departure = draw_departure(jax.random.fold_in(seeds[6], 71), 0)
    interp = bell_draw(seeds[2], (STEPS, NBLK, ROWS, ROWS), ROWS ** -0.5, 0.5, ((1, 256),))
    vertical_inv = draw_vertical_inv(jax.random.fold_in(seeds[6], 71), 0)
    regime = touch_ends(jax.random.randint(seeds[4], (NBLK, ROWS), 0, NSET), jax.random.fold_in(seeds[4], 1), 0, NSET - 1).astype(jnp.int32)
    bed_rate = jnp.clip(jnp.exp(jax.random.uniform(seeds[5], (CLASSES,), jnp.float32, math.log(0.3), math.log(1.5))), 0.3, 1.5)
    return dict(cotangent=cotangent, departure=departure, interp=interp, vertical_inv=vertical_inv, regime=regime, bed_rate=bed_rate)


def vertical(operators, regime, field):
    result = jnp.zeros(field.shape, jnp.float32)
    for regime_index in range(NSET):
        applied = jnp.einsum('ml,bmi->bli', operators[regime_index], field, precision=lax.Precision.HIGHEST)
        result = result + jnp.where(regime[:, None, :] == regime_index, applied, jnp.float32(0.0))
    return result


def reference(cotangent, departure, interp, vertical_inv, regime, bed_rate):
    field = cotangent
    for step_index in range(STEPS - 1, -1, -1):
        bottom = jnp.sum(bed_rate[:, None, None] * field[:, :, LAYERS - 1, :], axis=0)
        field = field.at[:, :, LAYERS - 1, :].add(bottom[None])
        adjoint = jnp.stack([vertical(vertical_inv[class_index], regime, field[class_index]) for class_index in range(CLASSES)]).astype(jnp.bfloat16)
        weights = interp[step_index].astype(jnp.float32)
        products = jnp.einsum('cbli,bij->cblj', adjoint.astype(jnp.float32), weights)
        routes = departure[step_index]
        field = jnp.stack([jax.ops.segment_sum(products[class_index], routes, num_segments=NBLK) for class_index in range(CLASSES)])
    return field
```

```python
import jax
import jax.numpy as jnp
from jax import lax
from jax.experimental import pallas as pl
from jax.experimental.pallas import tpu as pltpu
from jax.sharding import PartitionSpec as P

CELLS = 64
CLS = 4
BLOCKS = 128
OWN = BLOCKS // CLS
LAYERS = 24
COLS = 128
NSET = 4
REACH = 4
CAP = 32
STEPS = 2
CHUNK = 8
CHUNKS = LAYERS // CHUNK
ORDER = (2, 1, 0)
ROWS = CHUNK * OWN
MESH = pl.DeviceIdType.MESH
F32 = jnp.float32
BF16 = jnp.bfloat16


def iota(shape, dim):
    return lax.broadcasted_iota(jnp.int32, shape, dim)


def ones_where(mask):
    return jnp.where(mask, F32(1.0), F32(0.0)).astype(BF16)


def nt_dot(a, b, **kw):
    return lax.dot_general(a, b, (((1,), (1,)), ((), ())), preferred_element_type=F32, **kw)


def build_operators(v_ref, lhs, cls):
    eye = jnp.where(iota((LAYERS, LAYERS), 0) == iota((LAYERS, LAYERS), 1), F32(1.0), F32(0.0))
    shape = (LAYERS, 4 * LAYERS)
    col, row = iota(shape, 1), iota(shape, 0)
    place_high = ones_where((col == row) | (col == row + LAYERS))
    place_low = ones_where((col == row + 2 * LAYERS) | (col == row + 3 * LAYERS))
    parts = []
    for r in range(NSET):
        turned = nt_dot(eye, v_ref[cls, r], precision=lax.Precision.HIGHEST)
        high = turned.astype(BF16)
        low = (turned - high.astype(F32)).astype(BF16)
        parts.append(
            jnp.dot(high, place_high, preferred_element_type=F32)
            + jnp.dot(low, place_low, preferred_element_type=F32)
        )
    lhs[...] = jnp.concatenate(parts, axis=0).astype(BF16)


def route(dep, s, q):
    row = dep[s : s + 1, pl.ds(pl.multiple_of(q * BLOCKS, BLOCKS), BLOCKS)]
    off = q - (row >> 7)
    tgt = row & (BLOCKS - 1)
    hot = jnp.where(iota((16, BLOCKS), 0) == off, F32(1.0), F32(0.0))
    tri = ones_where(iota((BLOCKS, BLOCKS), 0) < iota((BLOCKS, BLOCKS), 1))
    before = jnp.dot(hot.astype(BF16), tri, preferred_element_type=F32)
    rank = jnp.sum(before * hot, axis=0, keepdims=True).astype(jnp.int32)
    slot = jnp.where(off > 0, (off - 1) * CAP + rank, -1)
    return off, tgt, slot


def build_tables(dep, gather, total, s, me):
    square = (BLOCKS, BLOCKS)
    off, tgt, slot = route(dep, s, me)
    gather[s] = ones_where(iota(square, 0) == slot)
    total[s, :, :BLOCKS] = ones_where(iota(square, 0) == jnp.where(off == 0, tgt, -1))
    remote = jnp.zeros(square, F32)
    for d in range(1, REACH + 1):
        off, tgt, slot = route(dep, s, lax.rem(me + d, CELLS))
        aims = ones_where(iota(square, 0) == tgt)
        slots = ones_where(iota(square, 0) == jnp.where(off == d, slot, -1))
        remote = remote + nt_dot(aims, slots)
    total[s, :, BLOCKS:] = remote.astype(BF16)


def kernel(
    cot, dep, w, v_ref, reg, rate, out,
    adj, ra, sb, pr, xs, xr, fs, pf, bed_out, bed_in, bot, lhs, gather, total,
    bed_s, bed_r, a1_s, a1_r, a2_s, a2_r, x_s, x_r,
):
    me = lax.axis_index("cells")
    cls = lax.axis_index("cls")

    def over_y(k):
        return (me, lax.rem(cls + k, CLS))

    def along(d):
        return (lax.rem(me + d + CELLS, CELLS), cls)

    barrier = pltpu.get_barrier_semaphore()
    partners = [over_y(k) for k in range(1, CLS)]
    partners += [along(d) for d in range(-REACH, REACH + 1) if d != 0]
    for partner in partners:
        pl.semaphore_signal(barrier, inc=1, device_id=partner, device_id_type=MESH)

    pending = []

    def send(src, dst, ssem, rsem, device):
        copy = pltpu.make_async_remote_copy(
            src_ref=src, dst_ref=dst, send_sem=ssem, recv_sem=rsem,
            device_id=device, device_id_type=MESH,
        )
        copy.start()
        pending.append(copy)
        return copy

    build_operators(v_ref, lhs, cls)
    my_rate = rate[cls]

    def send_bed(s):
        return [
            send(bed_out.at[s], bed_in.at[s, k - 1], bed_s.at[s, k - 1], bed_r.at[s, k - 1], over_y(k))
            for k in range(1, CLS)
        ]

    def bottom_of(s, copies):
        for copy in copies:
            copy.wait_recv()
        return bed_out[s] + bed_in[s, 0] + bed_in[s, 1] + bed_in[s, 2]

    def vertical(s, load, dest):
        def body(n, carry):
            b = dest * OWN + 2 * n
            field = jnp.concatenate([load(b), load(b + 1)], axis=1)
            high = field.astype(BF16).astype(F32)
            low = field - high
            rhs = jnp.concatenate([high, low, high, low], axis=0).astype(BF16)
            res = jnp.dot(lhs[...], rhs, preferred_element_type=F32)
            r = jnp.concatenate([reg[pl.ds(b, 1), :], reg[pl.ds(b + 1, 1), :]], axis=1)
            picked = res[:LAYERS]
            for i in range(1, NSET):
                picked = jnp.where(r == i, res[i * LAYERS : (i + 1) * LAYERS], picked)
            at = pl.ds(pl.multiple_of(n * 16, 16), 16)
            for lc in range(CHUNKS):
                part = picked[lc * CHUNK : (lc + 1) * CHUNK]
                both = jnp.concatenate([part[:, :COLS], part[:, COLS:]], axis=0)
                adj[s, lc, dest, at, :] = both.astype(BF16)
            return carry

        lax.fori_loop(0, OWN // 2, body, 0)

    def interpolate(s, lc):
        def body(n, carry):
            at = pl.ds(pl.multiple_of(n * 16, 16), 16)
            tiles = [adj[s, lc, cls, at, :]] + [ra[s, lc, k, at, :] for k in range(CLS - 1)]
            weights = jnp.concatenate([w[s, 2 * n], w[s, 2 * n + 1]], axis=1)
            res = jnp.dot(jnp.concatenate(tiles, axis=0), weights, preferred_element_type=F32)
            for k in range(CLS):
                pf[k, pl.ds(2 * n, CHUNK, stride=OWN), :] = res[k * 16 : k * 16 + 8, :COLS]
                pf[k, pl.ds(2 * n + 1, CHUNK, stride=OWN), :] = res[k * 16 + 8 : k * 16 + 16, COLS:]
            return carry

        lax.fori_loop(0, OWN // 2, body, 0)
        for k in range(1, CLS):
            sb[s, lc, k - 1] = pf[k].astype(BF16)
        pr[s, lc, cls] = pf[0].astype(BF16)

    def plane_of(s, lc, at):
        return jnp.concatenate([pr[s, lc, y, at, :] for y in range(CLS)], axis=0)

    def pack(s, lc):
        def body(n, carry):
            ats = [pl.ds(pl.multiple_of((2 * n + i) * OWN, OWN), OWN) for i in range(2)]
            rhs = jnp.concatenate([plane_of(s, lc, at) for at in ats], axis=1)
            res = jnp.dot(gather[s], rhs, preferred_element_type=F32).astype(BF16)
            for d in range(REACH):
                for i, at in enumerate(ats):
                    xs[s, lc, d, at, :] = res[d * CAP : (d + 1) * CAP, i * COLS : (i + 1) * COLS]
            return carry

        lax.fori_loop(0, CHUNK // 2, body, 0)

    def accumulate(s, lc, dst):
        def body(n, carry):
            ats = [pl.ds(pl.multiple_of((2 * n + i) * OWN, OWN), OWN) for i in range(2)]
            cols = [
                jnp.concatenate(
                    [plane_of(s, lc, at)] + [xr[s, lc, d, at, :] for d in range(REACH)], axis=0
                )
                for at in ats
            ]
            res = jnp.dot(total[s], jnp.concatenate(cols, axis=1), preferred_element_type=F32)
            for i in range(2):
                at = pl.multiple_of((lc * CHUNK + 2 * n + i) * BLOCKS, BLOCKS)
                dst[pl.ds(at, BLOCKS), :] = res[:, i * COLS : (i + 1) * COLS]
            return carry

        lax.fori_loop(0, CHUNK // 2, body, 0)

    first = STEPS - 1
    bed_out[first] = my_rate * cot[:, LAYERS - 1, :]
    pl.semaphore_wait(barrier, len(partners))
    beds = send_bed(first)
    for s in range(STEPS):
        build_tables(dep, gather, total, s, me)

    for s in range(STEPS - 1, -1, -1):
        if s == first:
            bot[...] = bottom_of(s, beds)
            last = iota((LAYERS, COLS), 0) == LAYERS - 1

            def load(b):
                return cot[b] + jnp.where(last, bot[pl.ds(b, 1), :], F32(0.0))
        else:
            tail = pl.ds((LAYERS - 1) * BLOCKS, BLOCKS)
            fs[tail, :] = fs[tail, :] + bottom_of(s, beds)

            def load(b):
                return fs[pl.ds(b, LAYERS, stride=BLOCKS), :]

        a1 = {}

        def send_adjoint(lc, k):
            a1[lc, k] = send(
                adj.at[s, lc, lax.rem(cls + k, CLS)], ra.at[s, lc, k - 1],
                a1_s.at[s, lc, k - 1], a1_r.at[s, lc, k - 1], over_y(k),
            )

        for k in (2, 1, 3):
            vertical(s, load, lax.rem(cls + k, CLS))
            send_adjoint(ORDER[0], k)
        for lc in ORDER[1:]:
            for k in (2, 1, 3):
                send_adjoint(lc, k)
        vertical(s, load, cls)

        a2 = {}
        for lc in ORDER:
            for k in range(1, CLS):
                a1[lc, k].wait_recv()
            interpolate(s, lc)
            for k in range(1, CLS):
                a2[lc, k] = send(
                    sb.at[s, lc, k - 1], pr.at[s, lc, cls],
                    a2_s.at[s, lc, k - 1], a2_r.at[s, lc, k - 1], over_y(CLS - k),
                )
        x = {}
        for lc in ORDER:
            for k in range(1, CLS):
                a2[lc, k].wait_recv()
            pack(s, lc)
            for d in range(REACH, 0, -1):
                x[lc, d] = send(
                    xs.at[s, lc, d - 1], xr.at[s, lc, d - 1],
                    x_s.at[s, lc, d - 1], x_r.at[s, lc, d - 1], along(-d),
                )
        for lc in ORDER:
            for d in range(1, REACH + 1):
                x[lc, d].wait_recv()
            accumulate(s, lc, fs if s > 0 else out)
            if s > 0 and lc == ORDER[0]:
                bed_out[s - 1] = my_rate * fs[pl.ds((LAYERS - 1) * BLOCKS, BLOCKS), :]
                beds = send_bed(s - 1)

    for copy in pending:
        copy.wait_send()


def local(cotangent, departure, interp, vertical_inv, regime, bed_rate):
    vmem = pl.BlockSpec(memory_space=pltpu.VMEM)
    dma = pltpu.SemaphoreType.DMA
    result = pl.pallas_call(
        kernel,
        out_shape=jax.ShapeDtypeStruct((LAYERS * BLOCKS, COLS), F32),
        in_specs=[vmem] * 5 + [pl.BlockSpec(memory_space=pltpu.SMEM)],
        out_specs=vmem,
        scratch_shapes=[
            pltpu.VMEM((STEPS, CHUNKS, CLS, ROWS, COLS), BF16),
            pltpu.VMEM((STEPS, CHUNKS, CLS - 1, ROWS, COLS), BF16),
            pltpu.VMEM((STEPS, CHUNKS, CLS - 1, ROWS, COLS), BF16),
            pltpu.VMEM((STEPS, CHUNKS, CLS, ROWS, COLS), BF16),
            pltpu.VMEM((STEPS, CHUNKS, REACH, ROWS, COLS), BF16),
            pltpu.VMEM((STEPS, CHUNKS, REACH, ROWS, COLS), BF16),
            pltpu.VMEM((LAYERS * BLOCKS, COLS), F32),
            pltpu.VMEM((CLS, ROWS, COLS), F32),
            pltpu.VMEM((STEPS, BLOCKS, COLS), F32),
            pltpu.VMEM((STEPS, CLS - 1, BLOCKS, COLS), F32),
            pltpu.VMEM((BLOCKS, COLS), F32),
            pltpu.VMEM((NSET * LAYERS, 4 * LAYERS), BF16),
            pltpu.VMEM((STEPS, BLOCKS, BLOCKS), BF16),
            pltpu.VMEM((STEPS, BLOCKS, 2 * BLOCKS), BF16),
            dma((STEPS, CLS - 1)),
            dma((STEPS, CLS - 1)),
            dma((STEPS, CHUNKS, CLS - 1)),
            dma((STEPS, CHUNKS, CLS - 1)),
            dma((STEPS, CHUNKS, CLS - 1)),
            dma((STEPS, CHUNKS, CLS - 1)),
            dma((STEPS, CHUNKS, REACH)),
            dma((STEPS, CHUNKS, REACH)),
        ],
        compiler_params=pltpu.CompilerParams(
            collective_id=0, has_side_effects=True, vmem_limit_bytes=40 * 1024 * 1024
        ),
        cost_estimate=pl.CostEstimate(flops=2_000_000_000, bytes_accessed=6_000_000, transcendentals=0),
    )(cotangent[0], departure, interp, vertical_inv, regime, bed_rate)
    return jnp.swapaxes(result.reshape(LAYERS, BLOCKS, COLS), 0, 1)[None]


def solution(mesh):
    placed = (
        P("cls", "cells", None, None),
        P(),
        P(None, ("cells", "cls"), None, None),
        P(),
        P("cells", None),
        P(),
    )
    return jax.shard_map(
        local, mesh=mesh, in_specs=placed, out_specs=P("cls", "cells", None, None), check_vma=False
    )
```

```python
import jax
import jax.numpy as jnp
from jax import lax
from jax.experimental import pallas as pl
from jax.experimental.pallas import tpu as pltpu
from jax.sharding import PartitionSpec as P

CELLS = 64
CLS = 4
BLOCKS = 128
OWN = BLOCKS // CLS
LAYERS = 24
COLS = 128
NSET = 4
REACH = 4
CAP = 32
STEPS = 2
CHUNK = 8
CHUNKS = LAYERS // CHUNK
ORDER = (2, 1, 0)
DESTS = (2, 1, 3, 0)
X_CHIPS = 4
ROWS = CHUNK * OWN
HALF = ROWS // 2
DIRECT = ((0, 0), (0, 1))
V_PAIRS = 16
I_PAIRS = 16
MESH = pl.DeviceIdType.MESH
F32 = jnp.float32
BF16 = jnp.bfloat16


def iota(shape, dim):
    return lax.broadcasted_iota(jnp.int32, shape, dim)


def ones_where(mask):
    return jnp.where(mask, F32(1.0), F32(0.0)).astype(BF16)


def nt_dot(a, b, **kw):
    return lax.dot_general(a, b, (((1,), (1,)), ((), ())), preferred_element_type=F32, **kw)


def build_operators(v_ref, lhs, cls):
    eye = jnp.where(iota((LAYERS, LAYERS), 0) == iota((LAYERS, LAYERS), 1), F32(1.0), F32(0.0))
    shape = (LAYERS, 4 * LAYERS)
    col, row = iota(shape, 1), iota(shape, 0)
    place_high = ones_where((col == row) | (col == row + LAYERS))
    place_low = ones_where((col == row + 2 * LAYERS) | (col == row + 3 * LAYERS))
    parts = []
    for r in range(NSET):
        turned = nt_dot(eye, v_ref[cls, r], precision=lax.Precision.HIGHEST)
        high = turned.astype(BF16)
        low = (turned - high.astype(F32)).astype(BF16)
        parts.append(
            jnp.dot(high, place_high, preferred_element_type=F32)
            + jnp.dot(low, place_low, preferred_element_type=F32)
        )
    lhs[...] = jnp.concatenate(parts, axis=0).astype(BF16)


def route(dep, s, q):
    row = dep[s : s + 1, pl.ds(pl.multiple_of(q * BLOCKS, BLOCKS), BLOCKS)]
    off = q - (row >> 7)
    tgt = row & (BLOCKS - 1)
    hot = jnp.where(iota((16, BLOCKS), 0) == off, F32(1.0), F32(0.0))
    tri = ones_where(iota((BLOCKS, BLOCKS), 0) < iota((BLOCKS, BLOCKS), 1))
    before = jnp.dot(hot.astype(BF16), tri, preferred_element_type=F32)
    rank = jnp.sum(before * hot, axis=0, keepdims=True).astype(jnp.int32)
    slot = jnp.where(off > 0, (off - 1) * CAP + rank, -1)
    return off, tgt, slot


def build_tables(dep, gather, total, s, me):
    square = (BLOCKS, BLOCKS)
    off, tgt, slot = route(dep, s, me)
    gather[s] = ones_where(iota(square, 0) == slot)
    total[s, :, :BLOCKS] = ones_where(iota(square, 0) == jnp.where(off == 0, tgt, -1))
    remote = jnp.zeros(square, F32)
    for d in range(1, REACH + 1):
        off, tgt, slot = route(dep, s, lax.rem(me + d, CELLS))
        aims = ones_where(iota(square, 0) == tgt)
        slots = ones_where(iota(square, 0) == jnp.where(off == d, slot, -1))
        remote = remote + nt_dot(aims, slots)
    total[s, :, BLOCKS:] = remote.astype(BF16)


def x_shift(p, by):
    x = (p // 2) % X_CHIPS
    return p + 2 * ((x + by + X_CHIPS) % X_CHIPS - x)


def kernel(
    cot_hbm, dep_hbm, w_hbm, v_hbm, reg_hbm, rate, out,
    cot, dep, w, v_ref, reg, adj, ra, sb, pr, xs, xr, rl, fs, pf, bed_out, bed_in, bot, lhs,
    gather, total, load_sem, out_sem, bed_s, bed_r, a1_s, a1_r, a2_s, a2_r, x_s, x_r, rl_s, rl_r,
):
    me = lax.axis_index("cells")
    cls = lax.axis_index("cls")

    split = LAYERS - CHUNK
    arrays = [
        (cot_hbm.at[:, split:, :], cot.at[:, split:, :]),
        (cot_hbm.at[:, :split, :], cot.at[:, :split, :]),
        (v_hbm, v_ref),
        (reg_hbm, reg),
        (dep_hbm, dep),
        (w_hbm, w),
    ]
    loads = [
        pltpu.make_async_copy(src, dst, load_sem.at[i]) for i, (src, dst) in enumerate(arrays)
    ]
    for copy in loads:
        copy.start()

    def over_y(k):
        return (me, lax.rem(cls + k, CLS))

    def along(d):
        return (lax.rem(me + d + CELLS, CELLS), cls)

    relay = (x_shift(me, 1), cls)
    relay_of = (x_shift(me, -1), cls)
    final = (lax.rem(x_shift(me, -1) - REACH + CELLS, CELLS), cls)
    final_of = (x_shift(lax.rem(me + REACH, CELLS), 1), cls)

    barrier = pltpu.get_barrier_semaphore()
    partners = [over_y(k) for k in range(1, CLS)]
    partners += [along(d) for d in range(-REACH, REACH + 1) if d != 0]
    partners += [relay, relay_of, final, final_of]
    for partner in partners:
        pl.semaphore_signal(barrier, inc=1, device_id=partner, device_id_type=MESH)

    pending = []

    def send(src, dst, ssem, rsem, device):
        copy = pltpu.make_async_remote_copy(
            src_ref=src, dst_ref=dst, send_sem=ssem, recv_sem=rsem,
            device_id=device, device_id_type=MESH,
        )
        copy.start()
        pending.append(copy)
        return copy

    my_rate = rate[cls]

    def own_rows(dest):
        return pl.ds(pl.multiple_of(dest * OWN, OWN), OWN)

    def send_bed(s):
        copies = {}
        for i in DESTS:
            for k in range(1, CLS):
                at = own_rows(lax.rem(cls + k + i, CLS))
                copies[i, k] = send(
                    bed_out.at[s, at], bed_in.at[s, k - 1, at],
                    bed_s.at[s, i, k - 1], bed_r.at[s, i, k - 1], over_y(k),
                )
        return copies

    def bottom_of(s, copies, i, dest):
        at = own_rows(dest)
        for k in range(1, CLS):
            copies[i, k].wait_recv()
        return bed_out[s, at] + bed_in[s, 0, at] + bed_in[s, 1, at] + bed_in[s, 2, at]

    def vertical(s, load, dest):
        def operands(b):
            field = jnp.concatenate([load(b), load(b + 1)], axis=1)
            high = field.astype(BF16).astype(F32)
            low = field - high
            return jnp.concatenate([high, low, high, low], axis=0).astype(BF16)

        def pick(b, res):
            r = jnp.concatenate([reg[pl.ds(b, 1), :], reg[pl.ds(b + 1, 1), :]], axis=1)
            picked = res[:LAYERS]
            for i in range(1, NSET):
                picked = jnp.where(r == i, res[i * LAYERS : (i + 1) * LAYERS], picked)
            return picked

        def body(g, carry):
            ns = [g * V_PAIRS + i for i in range(V_PAIRS)]
            bs = [dest * OWN + 2 * n for n in ns]
            rhs = [operands(b) for b in bs]
            res = [jnp.dot(lhs[...], x, preferred_element_type=F32) for x in rhs]
            for n, b, x in zip(ns, bs, res):
                picked = pick(b, x)
                at = pl.ds(pl.multiple_of(n * 16, 16), 16)
                for lc in range(CHUNKS):
                    part = picked[lc * CHUNK : (lc + 1) * CHUNK]
                    both = jnp.concatenate([part[:, :COLS], part[:, COLS:]], axis=0)
                    adj[s, lc, dest, at, :] = both.astype(BF16)
            return carry

        lax.fori_loop(0, OWN // 2 // V_PAIRS, body, 0)

    def interpolate(s, lc):
        def body(g, carry):
            ns = [g * I_PAIRS + i for i in range(I_PAIRS)]
            res = []
            for n in ns:
                at = pl.ds(pl.multiple_of(n * 16, 16), 16)
                tiles = [adj[s, lc, cls, at, :]] + [ra[s, lc, k, at, :] for k in range(CLS - 1)]
                weights = jnp.concatenate([w[s, 2 * n], w[s, 2 * n + 1]], axis=1)
                res.append(
                    jnp.dot(jnp.concatenate(tiles, axis=0), weights, preferred_element_type=F32)
                )
            for n, x in zip(ns, res):
                for k in range(CLS):
                    pf[k, pl.ds(2 * n, CHUNK, stride=OWN), :] = x[k * 16 : k * 16 + 8, :COLS]
                    pf[k, pl.ds(2 * n + 1, CHUNK, stride=OWN), :] = x[k * 16 + 8 : k * 16 + 16, COLS:]
            return carry

        lax.fori_loop(0, OWN // 2 // I_PAIRS, body, 0)
        for k in range(1, CLS):
            sb[s, lc, k - 1] = pf[k].astype(BF16)
        pr[s, lc, cls] = pf[0].astype(BF16)

    def plane_of(s, lc, at):
        return jnp.concatenate([pr[s, lc, y, at, :] for y in range(CLS)], axis=0)

    def pairs(lc, h):
        for n in range(CHUNK // 4):
            at = h * CHUNK // 2 + 2 * n
            yield [pl.ds((at + i) * OWN, OWN) for i in range(2)], lc * CHUNK + at

    def pack(s, lc, h):
        for ats, _ in pairs(lc, h):
            rhs = jnp.concatenate([plane_of(s, lc, at) for at in ats], axis=1)
            res = jnp.dot(gather[s], rhs, preferred_element_type=F32).astype(BF16)
            for d in range(REACH):
                for i, at in enumerate(ats):
                    xs[s, lc, d, at, :] = res[d * CAP : (d + 1) * CAP, i * COLS : (i + 1) * COLS]

    def accumulate(s, lc, h, dst):
        for ats, layer in pairs(lc, h):
            cols = [
                jnp.concatenate(
                    [plane_of(s, lc, at)] + [xr[s, lc, d, at, :] for d in range(REACH)], axis=0
                )
                for at in ats
            ]
            res = jnp.dot(total[s], jnp.concatenate(cols, axis=1), preferred_element_type=F32)
            for i in range(2):
                dst[pl.ds((layer + i) * BLOCKS, BLOCKS), :] = res[:, i * COLS : (i + 1) * COLS]

    first = STEPS - 1
    tail = (LAYERS - 1) * BLOCKS
    loads[0].wait()
    bed_out[first] = my_rate * cot[:, LAYERS - 1, :]
    pl.semaphore_wait(barrier, len(partners))
    beds = send_bed(first)
    for copy in loads[1:]:
        copy.wait()
    build_operators(v_ref, lhs, cls)

    stores = []
    for s in range(STEPS - 1, -1, -1):
        if s == first:
            last = iota((LAYERS, COLS), 0) == LAYERS - 1

            def add_bottom(i, dest):
                bot[own_rows(dest)] = bottom_of(s, beds, i, dest)

            def load(b):
                return cot[b] + jnp.where(last, bot[pl.ds(b, 1), :], F32(0.0))
        else:

            def add_bottom(i, dest):
                at = pl.ds(pl.multiple_of(tail + dest * OWN, OWN), OWN)
                fs[at, :] = fs[at, :] + bottom_of(s, beds, i, dest)

            def load(b):
                return fs[pl.ds(b, LAYERS, stride=BLOCKS), :]

        a1, a2, x, via = {}, {}, {}, {}

        def send_adjoint(lc, k):
            a1[lc, k] = send(
                adj.at[s, lc, lax.rem(cls + k, CLS)], ra.at[s, lc, k - 1],
                a1_s.at[s, lc, k - 1], a1_r.at[s, lc, k - 1], over_y(k),
            )

        def exchange(lc):
            for k in range(1, CLS):
                a1[lc, k].wait_recv()
            interpolate(s, lc)

        def rows(h):
            return pl.ds(h * HALF, HALF)

        def send_back(lc, h):
            for k in (2, 1, 3):
                a2[lc, h, k] = send(
                    sb.at[s, lc, k - 1, rows(h)], pr.at[s, lc, cls, rows(h)],
                    a2_s.at[s, lc, h, k - 1], a2_r.at[s, lc, h, k - 1], over_y(CLS - k),
                )

        def send_along(lc, h, d, src, device):
            x[lc, h, d] = send(
                src, xr.at[s, lc, d - 1, rows(h)],
                x_s.at[s, lc, h, d - 1], x_r.at[s, lc, h, d - 1], device,
            )

        def depart(lc, h):
            for k in range(1, CLS):
                a2[lc, h, k].wait_recv()
            pack(s, lc, h)
            far = xs.at[s, lc, REACH - 1, rows(h)]
            if (lc, h) in DIRECT:
                send_along(lc, h, REACH, far, along(-REACH))
            else:
                via[lc, h] = send(
                    far, rl.at[s, lc, rows(h)], rl_s.at[s, lc, h], rl_r.at[s, lc, h], relay
                )
            for d in range(REACH - 1, 0, -1):
                send_along(lc, h, d, xs.at[s, lc, d - 1, rows(h)], along(-d))

        def forward(lc, h):
            if (lc, h) not in DIRECT:
                via[lc, h].wait_recv()
                send_along(lc, h, REACH, rl.at[s, lc, rows(h)], final)

        def arrive(lc, h):
            for d in range(1, REACH + 1):
                x[lc, h, d].wait_recv()
            accumulate(s, lc, h, fs)
            if s == 0:
                size = HALF // OWN * BLOCKS
                at = pl.ds((lc * 2 + h) * size, size)
                copy = pltpu.make_async_copy(fs.at[at, :], out.at[at, :], out_sem.at[lc, h])
                copy.start()
                stores.append(copy)

        c0, c1, c2 = ORDER
        for i in DESTS:
            dest = lax.rem(cls + i, CLS)
            add_bottom(i, dest)
            vertical(s, load, dest)
            if i:
                send_adjoint(c0, i)
        for k in DESTS[:-1]:
            send_adjoint(c1, k)
        if s == first:
            for each in range(STEPS - 1, -1, -1):
                build_tables(dep, gather, total, each, me)
        exchange(c0)
        send_back(c0, 0)
        send_back(c0, 1)
        exchange(c1)
        send_back(c1, 0)
        for k in DESTS[:-1]:
            send_adjoint(c2, k)
        send_back(c1, 1)
        depart(c0, 0)
        depart(c0, 1)
        forward(c0, 0)
        depart(c1, 0)
        forward(c0, 1)
        exchange(c2)
        send_back(c2, 0)
        send_back(c2, 1)
        depart(c1, 1)
        forward(c1, 0)
        arrive(c0, 0)
        arrive(c0, 1)
        depart(c2, 0)
        forward(c1, 1)
        depart(c2, 1)
        if s > 0:
            bed_out[s - 1] = my_rate * fs[pl.ds(tail, BLOCKS), :]
            beds = send_bed(s - 1)
        forward(c2, 0)
        arrive(c1, 0)
        arrive(c1, 1)
        forward(c2, 1)
        arrive(c2, 0)
        arrive(c2, 1)

    for copy in pending:
        copy.wait_send()
    for copy in stores:
        copy.wait()


def local(cotangent, departure, interp, vertical_inv, regime, bed_rate):
    hbm = pl.BlockSpec(memory_space=pltpu.HBM)
    dma = pltpu.SemaphoreType.DMA
    result = pl.pallas_call(
        kernel,
        out_shape=jax.ShapeDtypeStruct((LAYERS * BLOCKS, COLS), F32),
        in_specs=[hbm] * 5 + [pl.BlockSpec(memory_space=pltpu.SMEM)],
        out_specs=hbm,
        scratch_shapes=[
            pltpu.VMEM((BLOCKS, LAYERS, COLS), F32),
            pltpu.VMEM((STEPS, CELLS * BLOCKS), jnp.int32),
            pltpu.VMEM((STEPS, OWN, COLS, COLS), BF16),
            pltpu.VMEM((CLS, NSET, LAYERS, LAYERS), F32),
            pltpu.VMEM((BLOCKS, COLS), jnp.int32),
            pltpu.VMEM((STEPS, CHUNKS, CLS, ROWS, COLS), BF16),
            pltpu.VMEM((STEPS, CHUNKS, CLS - 1, ROWS, COLS), BF16),
            pltpu.VMEM((STEPS, CHUNKS, CLS - 1, ROWS, COLS), BF16),
            pltpu.VMEM((STEPS, CHUNKS, CLS, ROWS, COLS), BF16),
            pltpu.VMEM((STEPS, CHUNKS, REACH, ROWS, COLS), BF16),
            pltpu.VMEM((STEPS, CHUNKS, REACH, ROWS, COLS), BF16),
            pltpu.VMEM((STEPS, CHUNKS, ROWS, COLS), BF16),
            pltpu.VMEM((LAYERS * BLOCKS, COLS), F32),
            pltpu.VMEM((CLS, ROWS, COLS), F32),
            pltpu.VMEM((STEPS, BLOCKS, COLS), F32),
            pltpu.VMEM((STEPS, CLS - 1, BLOCKS, COLS), F32),
            pltpu.VMEM((BLOCKS, COLS), F32),
            pltpu.VMEM((NSET * LAYERS, 4 * LAYERS), BF16),
            pltpu.VMEM((STEPS, BLOCKS, BLOCKS), BF16),
            pltpu.VMEM((STEPS, BLOCKS, 2 * BLOCKS), BF16),
            dma((6,)),
            dma((CHUNKS, 2)),
        ]
        + [dma((STEPS, CLS, CLS - 1))] * 2
        + [dma((STEPS, CHUNKS, CLS - 1))] * 2
        + [dma((STEPS, CHUNKS, 2, CLS - 1))] * 2
        + [dma((STEPS, CHUNKS, 2, REACH))] * 2
        + [dma((STEPS, CHUNKS, 2))] * 2,
        compiler_params=pltpu.CompilerParams(
            collective_id=0, has_side_effects=True, vmem_limit_bytes=56 * 1024 * 1024
        ),
        cost_estimate=pl.CostEstimate(flops=2_000_000_000, bytes_accessed=6_000_000, transcendentals=0),
    )(cotangent[0], departure, interp, vertical_inv, regime, bed_rate)
    return jnp.swapaxes(result.reshape(LAYERS, BLOCKS, COLS), 0, 1)[None]


def solution(mesh):
    placed = (
        P("cls", "cells", None, None),
        P(),
        P(None, ("cells", "cls"), None, None),
        P(),
        P("cells", None),
        P(),
    )
    return jax.shard_map(
        local, mesh=mesh, in_specs=placed, out_specs=P("cls", "cells", None, None), check_vma=False
    )
```

```python
import jax
import jax.numpy as jnp
from jax import lax
from jax.experimental import pallas as pl
from jax.experimental.pallas import tpu as pltpu
from jax.sharding import PartitionSpec as P

CELLS = 64
CLS = 4
BLOCKS = 128
OWN = BLOCKS // CLS
LAYERS = 24
COLS = 128
NSET = 4
REACH = 4
CAP = 32
STEPS = 2
CHUNK = 8
CHUNKS = LAYERS // CHUNK
ORDER = (2, 1, 0)
DESTS = (2, 1, 3, 0)
PIECES = 4
ROWS = CHUNK * OWN
HALF = ROWS // 2
V_PAIRS = 16
I_PAIRS = 16
MESH = pl.DeviceIdType.MESH
F32 = jnp.float32
BF16 = jnp.bfloat16


def iota(shape, dim):
    return lax.broadcasted_iota(jnp.int32, shape, dim)


def ones_where(mask):
    return jnp.where(mask, F32(1.0), F32(0.0)).astype(BF16)


def nt_dot(a, b, **kw):
    return lax.dot_general(a, b, (((1,), (1,)), ((), ())), preferred_element_type=F32, **kw)


def build_operators(v_ref, lhs, cls):
    eye = jnp.where(iota((LAYERS, LAYERS), 0) == iota((LAYERS, LAYERS), 1), F32(1.0), F32(0.0))
    shape = (LAYERS, 4 * LAYERS)
    col, row = iota(shape, 1), iota(shape, 0)
    place_high = ones_where((col == row) | (col == row + LAYERS))
    place_low = ones_where((col == row + 2 * LAYERS) | (col == row + 3 * LAYERS))
    parts = []
    for r in range(NSET):
        turned = nt_dot(eye, v_ref[cls, r], precision=lax.Precision.HIGHEST)
        high = turned.astype(BF16)
        low = (turned - high.astype(F32)).astype(BF16)
        parts.append(
            jnp.dot(high, place_high, preferred_element_type=F32)
            + jnp.dot(low, place_low, preferred_element_type=F32)
        )
    lhs[...] = jnp.concatenate(parts, axis=0).astype(BF16)


def route(dep, s, q):
    row = dep[s : s + 1, pl.ds(pl.multiple_of(q * BLOCKS, BLOCKS), BLOCKS)]
    off = q - (row >> 7)
    tgt = row & (BLOCKS - 1)
    hot = jnp.where(iota((16, BLOCKS), 0) == off, F32(1.0), F32(0.0))
    tri = ones_where(iota((BLOCKS, BLOCKS), 0) < iota((BLOCKS, BLOCKS), 1))
    before = jnp.dot(hot.astype(BF16), tri, preferred_element_type=F32)
    rank = jnp.sum(before * hot, axis=0, keepdims=True).astype(jnp.int32)
    slot = jnp.where(off > 0, (off - 1) * CAP + rank, -1)
    return off, tgt, slot


def build_tables(dep, gather, total, s, me):
    square = (BLOCKS, BLOCKS)
    off, tgt, slot = route(dep, s, me)
    gather[s] = ones_where(iota(square, 0) == slot)
    total[s, :, :BLOCKS] = ones_where(iota(square, 0) == jnp.where(off == 0, tgt, -1))
    remote = jnp.zeros(square, F32)
    for d in range(1, REACH + 1):
        off, tgt, slot = route(dep, s, lax.rem(me + d, CELLS))
        aims = ones_where(iota(square, 0) == tgt)
        slots = ones_where(iota(square, 0) == jnp.where(off == d, slot, -1))
        remote = remote + nt_dot(aims, slots)
    total[s, :, BLOCKS:] = remote.astype(BF16)


def kernel(
    cot_hbm, dep_hbm, w_hbm, v_hbm, reg_hbm, rate, out,
    cot, dep, w, v_ref, reg, adj, ra, sb, pr, xs, xr, fs, ob, pf, bed_out, bed_in, bot, lhs,
    gather, total, load_sem, out_sem, bed_s, bed_r, a1_s, a1_r, a2_s, a2_r, x_s, x_r,
):
    me = lax.axis_index("cells")
    cls = lax.axis_index("cls")

    split = LAYERS - CHUNK
    arrays = [
        (cot_hbm.at[:, split:, :], cot.at[:, split:, :]),
        (cot_hbm.at[:, :split, :], cot.at[:, :split, :]),
        (v_hbm, v_ref),
        (reg_hbm, reg),
        (dep_hbm, dep),
        (w_hbm, w),
    ]
    loads = [
        pltpu.make_async_copy(src, dst, load_sem.at[i]) for i, (src, dst) in enumerate(arrays)
    ]
    for copy in loads:
        copy.start()

    def over_y(k):
        return (me, lax.rem(cls + k, CLS))

    def along(d):
        return (lax.rem(me + d + CELLS, CELLS), cls)

    barrier = pltpu.get_barrier_semaphore()
    partners = [over_y(k) for k in range(1, CLS)]
    partners += [along(d) for d in range(-REACH, REACH + 1) if d != 0]
    for partner in partners:
        pl.semaphore_signal(barrier, inc=1, device_id=partner, device_id_type=MESH)

    pending = []

    def send(src, dst, ssem, rsem, device):
        copy = pltpu.make_async_remote_copy(
            src_ref=src, dst_ref=dst, send_sem=ssem, recv_sem=rsem,
            device_id=device, device_id_type=MESH,
        )
        copy.start()
        pending.append(copy)
        return copy

    my_rate = rate[cls]

    def own_rows(dest):
        return pl.ds(pl.multiple_of(dest * OWN, OWN), OWN)

    def send_bed(s):
        copies = {}
        for i in DESTS:
            for k in range(1, CLS):
                at = own_rows(lax.rem(cls + k + i, CLS))
                copies[i, k] = send(
                    bed_out.at[s, at], bed_in.at[s, k - 1, at],
                    bed_s.at[s, i, k - 1], bed_r.at[s, i, k - 1], over_y(k),
                )
        return copies

    def bottom_of(s, copies, i, dest):
        at = own_rows(dest)
        for k in range(1, CLS):
            copies[i, k].wait_recv()
        return bed_out[s, at] + bed_in[s, 0, at] + bed_in[s, 1, at] + bed_in[s, 2, at]

    def vertical(s, load, dest):
        def operands(b):
            field = jnp.concatenate([load(b), load(b + 1)], axis=1)
            high = field.astype(BF16).astype(F32)
            low = field - high
            return jnp.concatenate([high, low, high, low], axis=0).astype(BF16)

        def pick(b, res):
            r = jnp.concatenate([reg[pl.ds(b, 1), :], reg[pl.ds(b + 1, 1), :]], axis=1)
            picked = res[:LAYERS]
            for i in range(1, NSET):
                picked = jnp.where(r == i, res[i * LAYERS : (i + 1) * LAYERS], picked)
            return picked

        def body(g, carry):
            ns = [g * V_PAIRS + i for i in range(V_PAIRS)]
            bs = [dest * OWN + 2 * n for n in ns]
            rhs = [operands(b) for b in bs]
            res = [jnp.dot(lhs[...], x, preferred_element_type=F32) for x in rhs]
            for n, b, x in zip(ns, bs, res):
                picked = pick(b, x)
                at = pl.ds(pl.multiple_of(n * 16, 16), 16)
                for lc in range(CHUNKS):
                    part = picked[lc * CHUNK : (lc + 1) * CHUNK]
                    both = jnp.concatenate([part[:, :COLS], part[:, COLS:]], axis=0)
                    adj[s, lc, dest, at, :] = both.astype(BF16)
            return carry

        lax.fori_loop(0, OWN // 2 // V_PAIRS, body, 0)

    def interpolate(s, lc):
        def body(g, carry):
            ns = [g * I_PAIRS + i for i in range(I_PAIRS)]
            res = []
            for n in ns:
                at = pl.ds(pl.multiple_of(n * 16, 16), 16)
                tiles = [adj[s, lc, cls, at, :]] + [ra[s, lc, k, at, :] for k in range(CLS - 1)]
                weights = jnp.concatenate([w[s, 2 * n], w[s, 2 * n + 1]], axis=1)
                res.append(
                    jnp.dot(jnp.concatenate(tiles, axis=0), weights, preferred_element_type=F32)
                )
            for n, x in zip(ns, res):
                for k in range(CLS):
                    pf[k, pl.ds(2 * n, CHUNK, stride=OWN), :] = x[k * 16 : k * 16 + 8, :COLS]
                    pf[k, pl.ds(2 * n + 1, CHUNK, stride=OWN), :] = x[k * 16 + 8 : k * 16 + 16, COLS:]
            return carry

        lax.fori_loop(0, OWN // 2 // I_PAIRS, body, 0)
        for k in range(1, CLS):
            sb[s, lc, k - 1] = pf[k].astype(BF16)
        pr[s, lc, cls] = pf[0].astype(BF16)

    def plane_of(s, lc, at):
        return jnp.concatenate([pr[s, lc, y, at, :] for y in range(CLS)], axis=0)

    def pairs(lc, h):
        for n in range(CHUNK // 4):
            at = h * CHUNK // 2 + 2 * n
            yield [pl.ds((at + i) * OWN, OWN) for i in range(2)], lc * CHUNK + at

    def pack(s, lc, h):
        for ats, _ in pairs(lc, h):
            rhs = jnp.concatenate([plane_of(s, lc, at) for at in ats], axis=1)
            res = jnp.dot(gather[s], rhs, preferred_element_type=F32).astype(BF16)
            for d in range(REACH):
                for i, at in enumerate(ats):
                    xs[s, lc, d, at, :] = res[d * CAP : (d + 1) * CAP, i * COLS : (i + 1) * COLS]

    def accumulate(s, lc, h, dst, place):
        for ats, layer in pairs(lc, h):
            cols = [
                jnp.concatenate(
                    [plane_of(s, lc, at)] + [xr[s, lc, d, at, :] for d in range(REACH)], axis=0
                )
                for at in ats
            ]
            res = jnp.dot(total[s], jnp.concatenate(cols, axis=1), preferred_element_type=F32)
            for i in range(2):
                dst[place(layer + i), :] = res[:, i * COLS : (i + 1) * COLS]

    first = STEPS - 1
    tail = (LAYERS - 1) * BLOCKS
    loads[0].wait()
    bed_out[first] = my_rate * cot[:, LAYERS - 1, :]
    pl.semaphore_wait(barrier, len(partners))
    beds = send_bed(first)
    for copy in loads[1:]:
        copy.wait()
    build_operators(v_ref, lhs, cls)

    stores = []
    for s in range(STEPS - 1, -1, -1):
        if s == first:
            last = iota((LAYERS, COLS), 0) == LAYERS - 1

            def add_bottom(i, dest):
                bot[own_rows(dest)] = bottom_of(s, beds, i, dest)

            def load(b):
                return cot[b] + jnp.where(last, bot[pl.ds(b, 1), :], F32(0.0))
        else:

            def add_bottom(i, dest):
                at = pl.ds(pl.multiple_of(tail + dest * OWN, OWN), OWN)
                fs[at, :] = fs[at, :] + bottom_of(s, beds, i, dest)

            def load(b):
                return fs[pl.ds(b, LAYERS, stride=BLOCKS), :]

        a1, a2, x = {}, {}, {}

        def send_adjoint(lc, k):
            a1[lc, k] = send(
                adj.at[s, lc, lax.rem(cls + k, CLS)], ra.at[s, lc, k - 1],
                a1_s.at[s, lc, k - 1], a1_r.at[s, lc, k - 1], over_y(k),
            )

        def exchange(lc):
            for k in range(1, CLS):
                a1[lc, k].wait_recv()
            interpolate(s, lc)

        def rows(h):
            return pl.ds(h * HALF, HALF)

        def send_back(lc, h):
            for k in (2, 1, 3):
                a2[lc, h, k] = send(
                    sb.at[s, lc, k - 1, rows(h)], pr.at[s, lc, cls, rows(h)],
                    a2_s.at[s, lc, h, k - 1], a2_r.at[s, lc, h, k - 1], over_y(CLS - k),
                )

        def depart(lc, h):
            for k in range(1, CLS):
                a2[lc, h, k].wait_recv()
            pack(s, lc, h)
            for d in range(REACH, 0, -1):
                x[lc, h, d] = send(
                    xs.at[s, lc, d - 1, rows(h)], xr.at[s, lc, d - 1, rows(h)],
                    x_s.at[s, lc, h, d - 1], x_r.at[s, lc, h, d - 1], along(-d),
                )

        def arrive(lc, h):
            for d in range(1, REACH + 1):
                x[lc, h, d].wait_recv()
            if s > 0:
                accumulate(s, lc, h, fs, lambda layer: pl.ds(layer * BLOCKS, BLOCKS))
                return
            accumulate(s, lc, h, ob, lambda layer: pl.ds(layer, BLOCKS, stride=LAYERS))
            if h == 1:
                at = pl.ds(lc * CHUNK, CHUNK)
                copy = pltpu.make_async_copy(
                    ob.reshape(BLOCKS, LAYERS, COLS).at[:, at, :], out.at[:, at, :], out_sem.at[lc]
                )
                copy.start()
                stores.append(copy)

        c0, c1, c2 = ORDER
        for i in DESTS:
            dest = lax.rem(cls + i, CLS)
            add_bottom(i, dest)
            vertical(s, load, dest)
            if i:
                send_adjoint(c0, i)
        for k in DESTS[:-1]:
            send_adjoint(c1, k)
        if s == first:
            for each in range(STEPS - 1, -1, -1):
                build_tables(dep, gather, total, each, me)
        exchange(c0)
        send_back(c0, 0)
        send_back(c0, 1)
        exchange(c1)
        send_back(c1, 0)
        for k in DESTS[:-1]:
            send_adjoint(c2, k)
        send_back(c1, 1)
        depart(c0, 0)
        depart(c0, 1)
        depart(c1, 0)
        exchange(c2)
        send_back(c2, 0)
        send_back(c2, 1)
        depart(c1, 1)
        arrive(c0, 0)
        arrive(c0, 1)
        depart(c2, 0)
        depart(c2, 1)
        if s > 0:
            bed_out[s - 1] = my_rate * fs[pl.ds(tail, BLOCKS), :]
            beds = send_bed(s - 1)
        arrive(c1, 0)
        arrive(c1, 1)
        arrive(c2, 0)
        arrive(c2, 1)

    for copy in pending:
        copy.wait_send()
    for copy in stores:
        copy.wait()


def place_result(src, dst, held, in_sem, out_sem):
    size = BLOCKS // PIECES
    pieces = [pl.ds(i * size, size) for i in range(PIECES)]
    ins = [
        pltpu.make_async_copy(src.at[at], held.at[at], in_sem.at[i]) for i, at in enumerate(pieces)
    ]
    outs = [
        pltpu.make_async_copy(held.at[at], dst.at[at], out_sem.at[i]) for i, at in enumerate(pieces)
    ]
    for copy in ins:
        copy.start()
    for into, onward in zip(ins, outs):
        into.wait()
        onward.start()
    for copy in outs:
        copy.wait()


def local(cotangent, departure, interp, vertical_inv, regime, bed_rate):
    hbm = pl.BlockSpec(memory_space=pltpu.HBM)
    dma = pltpu.SemaphoreType.DMA
    result = pl.pallas_call(
        kernel,
        out_shape=jax.ShapeDtypeStruct((BLOCKS, LAYERS, COLS), F32),
        in_specs=[hbm] * 5 + [pl.BlockSpec(memory_space=pltpu.SMEM)],
        out_specs=hbm,
        scratch_shapes=[
            pltpu.VMEM((BLOCKS, LAYERS, COLS), F32),
            pltpu.VMEM((STEPS, CELLS * BLOCKS), jnp.int32),
            pltpu.VMEM((STEPS, OWN, COLS, COLS), BF16),
            pltpu.VMEM((CLS, NSET, LAYERS, LAYERS), F32),
            pltpu.VMEM((BLOCKS, COLS), jnp.int32),
            pltpu.VMEM((STEPS, CHUNKS, CLS, ROWS, COLS), BF16),
            pltpu.VMEM((STEPS, CHUNKS, CLS - 1, ROWS, COLS), BF16),
            pltpu.VMEM((STEPS, CHUNKS, CLS - 1, ROWS, COLS), BF16),
            pltpu.VMEM((STEPS, CHUNKS, CLS, ROWS, COLS), BF16),
            pltpu.VMEM((STEPS, CHUNKS, REACH, ROWS, COLS), BF16),
            pltpu.VMEM((STEPS, CHUNKS, REACH, ROWS, COLS), BF16),
            pltpu.VMEM((LAYERS * BLOCKS, COLS), F32),
            pltpu.VMEM((LAYERS * BLOCKS, COLS), F32),
            pltpu.VMEM((CLS, ROWS, COLS), F32),
            pltpu.VMEM((STEPS, BLOCKS, COLS), F32),
            pltpu.VMEM((STEPS, CLS - 1, BLOCKS, COLS), F32),
            pltpu.VMEM((BLOCKS, COLS), F32),
            pltpu.VMEM((NSET * LAYERS, 4 * LAYERS), BF16),
            pltpu.VMEM((STEPS, BLOCKS, BLOCKS), BF16),
            pltpu.VMEM((STEPS, BLOCKS, 2 * BLOCKS), BF16),
            dma((6,)),
            dma((CHUNKS,)),
        ]
        + [dma((STEPS, CLS, CLS - 1))] * 2
        + [dma((STEPS, CHUNKS, CLS - 1))] * 2
        + [dma((STEPS, CHUNKS, 2, CLS - 1))] * 2
        + [dma((STEPS, CHUNKS, 2, REACH))] * 2,
        compiler_params=pltpu.CompilerParams(
            collective_id=0, has_side_effects=True, vmem_limit_bytes=56 * 1024 * 1024
        ),
        cost_estimate=pl.CostEstimate(flops=2_000_000_000, bytes_accessed=6_000_000, transcendentals=0),
    )(cotangent[0], departure, interp, vertical_inv, regime, bed_rate)
    return pl.pallas_call(
        place_result,
        out_shape=jax.ShapeDtypeStruct((BLOCKS, LAYERS, COLS), F32),
        in_specs=[hbm],
        out_specs=hbm,
        scratch_shapes=[pltpu.VMEM((BLOCKS, LAYERS, COLS), F32), dma((PIECES,)), dma((PIECES,))],
        compiler_params=pltpu.CompilerParams(vmem_limit_bytes=56 * 1024 * 1024),
    )(result)[None]


def solution(mesh):
    placed = (
        P("cls", "cells", None, None),
        P(),
        P(None, ("cells", "cls"), None, None),
        P(),
        P("cells", None),
        P(),
    )
    return jax.shard_map(
        local, mesh=mesh, in_specs=placed, out_specs=P("cls", "cells", None, None), check_vma=False
    )
```

```python
import jax
import jax.numpy as jnp
from jax import lax
from jax.experimental import pallas as pl
from jax.experimental.pallas import tpu as pltpu
from jax.sharding import PartitionSpec as P

CELLS = 64
CLS = 4
BLOCKS = 128
OWN = BLOCKS // CLS
LAYERS = 24
COLS = 128
NSET = 4
REACH = 4
CAP = 32
STEPS = 2
CHUNK = 8
CHUNKS = LAYERS // CHUNK
ORDER = (2, 1, 0)
DESTS = (2, 1, 3, 0)
PIECES = 4
ROWS = CHUNK * OWN
STEP = OWN + 8
PITCH = BLOCKS + 8
HALF = ROWS // 2
V_PAIRS = 16
I_PAIRS = 16
MESH = pl.DeviceIdType.MESH
F32 = jnp.float32
BF16 = jnp.bfloat16


def iota(shape, dim):
    return lax.broadcasted_iota(jnp.int32, shape, dim)


def ones_where(mask):
    return jnp.where(mask, F32(1.0), F32(0.0)).astype(BF16)


def nt_dot(a, b, **kw):
    return lax.dot_general(a, b, (((1,), (1,)), ((), ())), preferred_element_type=F32, **kw)


def build_operators(v_ref, lhs, cls):
    eye = jnp.where(iota((LAYERS, LAYERS), 0) == iota((LAYERS, LAYERS), 1), F32(1.0), F32(0.0))
    shape = (LAYERS, 4 * LAYERS)
    col, row = iota(shape, 1), iota(shape, 0)
    place_high = ones_where((col == row) | (col == row + LAYERS))
    place_low = ones_where((col == row + 2 * LAYERS) | (col == row + 3 * LAYERS))
    parts = []
    for r in range(NSET):
        turned = nt_dot(eye, v_ref[cls, r], precision=lax.Precision.HIGHEST)
        high = turned.astype(BF16)
        low = (turned - high.astype(F32)).astype(BF16)
        parts.append(
            jnp.dot(high, place_high, preferred_element_type=F32)
            + jnp.dot(low, place_low, preferred_element_type=F32)
        )
    lhs[...] = jnp.concatenate(parts, axis=0).astype(BF16)


def route(dep, s, q):
    row = dep[s : s + 1, pl.ds(pl.multiple_of(q * BLOCKS, BLOCKS), BLOCKS)]
    off = q - (row >> 7)
    tgt = row & (BLOCKS - 1)
    hot = jnp.where(iota((16, BLOCKS), 0) == off, F32(1.0), F32(0.0))
    tri = ones_where(iota((BLOCKS, BLOCKS), 0) < iota((BLOCKS, BLOCKS), 1))
    before = jnp.dot(hot.astype(BF16), tri, preferred_element_type=F32)
    rank = jnp.sum(before * hot, axis=0, keepdims=True).astype(jnp.int32)
    slot = jnp.where(off > 0, (off - 1) * CAP + rank, -1)
    return off, tgt, slot


def build_tables(dep, gather, total, s, me):
    square = (BLOCKS, BLOCKS)
    off, tgt, slot = route(dep, s, me)
    gather[s] = ones_where(iota(square, 0) == slot)
    total[s, :, :BLOCKS] = ones_where(iota(square, 0) == jnp.where(off == 0, tgt, -1))
    remote = jnp.zeros(square, F32)
    for d in range(1, REACH + 1):
        off, tgt, slot = route(dep, s, lax.rem(me + d, CELLS))
        aims = ones_where(iota(square, 0) == tgt)
        slots = ones_where(iota(square, 0) == jnp.where(off == d, slot, -1))
        remote = remote + nt_dot(aims, slots)
    total[s, :, BLOCKS:] = remote.astype(BF16)


def kernel(
    cot_hbm, dep_hbm, w_hbm, v_hbm, reg_hbm, rate, out,
    cot, dep, w, v_ref, reg, adj, ra, sb, pr, xs, xr, fs, ob, pf, bed_out, bed_in, bot, lhs,
    gather, total, load_sem, out_sem, bed_s, bed_r, a1_s, a1_r, a2_s, a2_r, x_s, x_r,
):
    me = lax.axis_index("cells")
    cls = lax.axis_index("cls")

    split = LAYERS - CHUNK
    arrays = [
        (cot_hbm.at[:, split:, :], cot.at[:, split:, :]),
        (cot_hbm.at[:, :split, :], cot.at[:, :split, :]),
        (v_hbm, v_ref),
        (reg_hbm, reg),
        (dep_hbm, dep),
        (w_hbm, w),
    ]
    loads = [
        pltpu.make_async_copy(src, dst, load_sem.at[i]) for i, (src, dst) in enumerate(arrays)
    ]
    for copy in loads:
        copy.start()

    def over_y(k):
        return (me, lax.rem(cls + k, CLS))

    def along(d):
        return (lax.rem(me + d + CELLS, CELLS), cls)

    barrier = pltpu.get_barrier_semaphore()
    partners = [over_y(k) for k in range(1, CLS)]
    partners += [along(d) for d in range(-REACH, REACH + 1) if d != 0]
    for partner in partners:
        pl.semaphore_signal(barrier, inc=1, device_id=partner, device_id_type=MESH)

    pending = []

    def send(src, dst, ssem, rsem, device):
        copy = pltpu.make_async_remote_copy(
            src_ref=src, dst_ref=dst, send_sem=ssem, recv_sem=rsem,
            device_id=device, device_id_type=MESH,
        )
        copy.start()
        pending.append(copy)
        return copy

    my_rate = rate[cls]

    def own_rows(dest):
        return pl.ds(pl.multiple_of(dest * OWN, OWN), OWN)

    def send_bed(s):
        copies = {}
        for i in DESTS:
            for k in range(1, CLS):
                at = own_rows(lax.rem(cls + k + i, CLS))
                copies[i, k] = send(
                    bed_out.at[s, at], bed_in.at[s, k - 1, at],
                    bed_s.at[s, i, k - 1], bed_r.at[s, i, k - 1], over_y(k),
                )
        return copies

    def bottom_of(s, copies, i, dest):
        at = own_rows(dest)
        for k in range(1, CLS):
            copies[i, k].wait_recv()
        return bed_out[s, at] + bed_in[s, 0, at] + bed_in[s, 1, at] + bed_in[s, 2, at]

    def vertical(s, load, dest):
        def operands(b):
            field = jnp.concatenate([load(b), load(b + 1)], axis=1)
            high = field.astype(BF16).astype(F32)
            low = field - high
            return jnp.concatenate([high, low, high, low], axis=0).astype(BF16)

        def pick(b, res):
            r = jnp.concatenate([reg[pl.ds(b, 1), :], reg[pl.ds(b + 1, 1), :]], axis=1)
            picked = res[:LAYERS]
            for i in range(1, NSET):
                picked = jnp.where(r == i, res[i * LAYERS : (i + 1) * LAYERS], picked)
            return picked

        def body(g, carry):
            ns = [g * V_PAIRS + i for i in range(V_PAIRS)]
            bs = [dest * OWN + 2 * n for n in ns]
            rhs = [operands(b) for b in bs]
            res = [jnp.dot(lhs[...], x, preferred_element_type=F32) for x in rhs]
            for n, b, x in zip(ns, bs, res):
                picked = pick(b, x)
                at = pl.ds(pl.multiple_of(n * 16, 16), 16)
                for lc in range(CHUNKS):
                    part = picked[lc * CHUNK : (lc + 1) * CHUNK]
                    both = jnp.concatenate([part[:, :COLS], part[:, COLS:]], axis=0)
                    adj[s, lc, dest, at, :] = both.astype(BF16)
            return carry

        lax.fori_loop(0, OWN // 2 // V_PAIRS, body, 0)

    def interpolate(s, lc):
        def body(g, carry):
            ns = [g * I_PAIRS + i for i in range(I_PAIRS)]
            res = []
            for n in ns:
                at = pl.ds(pl.multiple_of(n * 16, 16), 16)
                tiles = [adj[s, lc, cls, at, :]] + [ra[s, lc, k, at, :] for k in range(CLS - 1)]
                weights = jnp.concatenate([w[s, 2 * n], w[s, 2 * n + 1]], axis=1)
                res.append(
                    jnp.dot(jnp.concatenate(tiles, axis=0), weights, preferred_element_type=F32)
                )
            for n, x in zip(ns, res):
                for k in range(CLS):
                    pf[k, pl.ds(2 * n, CHUNK, stride=STEP), :] = x[k * 16 : k * 16 + 8, :COLS]
                    pf[k, pl.ds(2 * n + 1, CHUNK, stride=STEP), :] = x[k * 16 + 8 : k * 16 + 16, COLS:]
            return carry

        lax.fori_loop(0, OWN // 2 // I_PAIRS, body, 0)
        for i in range(CHUNK):
            at, packed = pl.ds(i * STEP, OWN), pl.ds(i * OWN, OWN)
            for k in range(1, CLS):
                sb[s, lc, k - 1, packed, :] = pf[k, at, :].astype(BF16)
            pr[s, lc, cls, packed, :] = pf[0, at, :].astype(BF16)

    def plane_of(s, lc, at):
        return jnp.concatenate([pr[s, lc, y, at, :] for y in range(CLS)], axis=0)

    def pairs(lc, h):
        for n in range(CHUNK // 4):
            at = h * CHUNK // 2 + 2 * n
            yield [pl.ds((at + i) * OWN, OWN) for i in range(2)], lc * CHUNK + at

    def pack(s, lc, h):
        for ats, _ in pairs(lc, h):
            rhs = jnp.concatenate([plane_of(s, lc, at) for at in ats], axis=1)
            res = jnp.dot(gather[s], rhs, preferred_element_type=F32).astype(BF16)
            for d in range(REACH):
                for i, at in enumerate(ats):
                    xs[s, lc, d, at, :] = res[d * CAP : (d + 1) * CAP, i * COLS : (i + 1) * COLS]

    def accumulate(s, lc, h, dst, place):
        for ats, layer in pairs(lc, h):
            cols = [
                jnp.concatenate(
                    [plane_of(s, lc, at)] + [xr[s, lc, d, at, :] for d in range(REACH)], axis=0
                )
                for at in ats
            ]
            res = jnp.dot(total[s], jnp.concatenate(cols, axis=1), preferred_element_type=F32)
            for i in range(2):
                dst[place(layer + i), :] = res[:, i * COLS : (i + 1) * COLS]

    first = STEPS - 1
    tail = (LAYERS - 1) * PITCH
    loads[0].wait()
    bed_out[first] = my_rate * cot[:, LAYERS - 1, :]
    pl.semaphore_wait(barrier, len(partners))
    beds = send_bed(first)
    for copy in loads[1:]:
        copy.wait()
    build_operators(v_ref, lhs, cls)
    for s in range(STEPS):
        build_tables(dep, gather, total, s, me)

    stores = []
    for s in range(STEPS - 1, -1, -1):
        if s == first:
            last = iota((LAYERS, COLS), 0) == LAYERS - 1

            def add_bottom(i, dest):
                bot[own_rows(dest)] = bottom_of(s, beds, i, dest)

            def load(b):
                return cot[b] + jnp.where(last, bot[pl.ds(b, 1), :], F32(0.0))
        else:

            def add_bottom(i, dest):
                at = pl.ds(pl.multiple_of(tail + dest * OWN, 8), OWN)
                fs[at, :] = fs[at, :] + bottom_of(s, beds, i, dest)

            def load(b):
                return fs[pl.ds(b, LAYERS, stride=PITCH), :]

        a1, a2, x = {}, {}, {}

        def send_adjoint(lc, k):
            a1[lc, k] = send(
                adj.at[s, lc, lax.rem(cls + k, CLS)], ra.at[s, lc, k - 1],
                a1_s.at[s, lc, k - 1], a1_r.at[s, lc, k - 1], over_y(k),
            )

        def exchange(lc):
            for k in range(1, CLS):
                a1[lc, k].wait_recv()
            interpolate(s, lc)

        def rows(h):
            return pl.ds(h * HALF, HALF)

        def send_back(lc, h):
            for k in (2, 1, 3):
                a2[lc, h, k] = send(
                    sb.at[s, lc, k - 1, rows(h)], pr.at[s, lc, cls, rows(h)],
                    a2_s.at[s, lc, h, k - 1], a2_r.at[s, lc, h, k - 1], over_y(CLS - k),
                )

        def depart(lc, h):
            for k in range(1, CLS):
                a2[lc, h, k].wait_recv()
            pack(s, lc, h)
            for d in range(REACH, 0, -1):
                x[lc, h, d] = send(
                    xs.at[s, lc, d - 1, rows(h)], xr.at[s, lc, d - 1, rows(h)],
                    x_s.at[s, lc, h, d - 1], x_r.at[s, lc, h, d - 1], along(-d),
                )

        def arrive(lc, h):
            for d in range(1, REACH + 1):
                x[lc, h, d].wait_recv()
            if s > 0:
                accumulate(s, lc, h, fs, lambda layer: pl.ds(layer * PITCH, BLOCKS))
                return
            accumulate(s, lc, h, ob, lambda layer: pl.ds(layer, BLOCKS, stride=LAYERS))
            if h == 1:
                at = pl.ds(lc * CHUNK, CHUNK)
                copy = pltpu.make_async_copy(
                    ob.reshape(BLOCKS, LAYERS, COLS).at[:, at, :], out.at[:, at, :], out_sem.at[lc]
                )
                copy.start()
                stores.append(copy)

        c0, c1, c2 = ORDER
        for i in DESTS:
            dest = lax.rem(cls + i, CLS)
            add_bottom(i, dest)
            vertical(s, load, dest)
            if i:
                send_adjoint(c0, i)
        for k in DESTS[:-1]:
            send_adjoint(c1, k)
        exchange(c0)
        send_back(c0, 0)
        send_back(c0, 1)
        exchange(c1)
        send_back(c1, 0)
        for k in DESTS[:-1]:
            send_adjoint(c2, k)
        send_back(c1, 1)
        depart(c0, 0)
        depart(c0, 1)
        depart(c1, 0)
        exchange(c2)
        send_back(c2, 0)
        send_back(c2, 1)
        depart(c1, 1)
        arrive(c0, 0)
        arrive(c0, 1)
        if s > 0:
            bed_out[s - 1] = my_rate * fs[pl.ds(tail, BLOCKS), :]
            beds = send_bed(s - 1)
        depart(c2, 0)
        depart(c2, 1)
        arrive(c1, 0)
        arrive(c1, 1)
        arrive(c2, 0)
        arrive(c2, 1)

    for copy in pending:
        copy.wait_send()
    for copy in stores:
        copy.wait()


def place_result(src, dst, held, in_sem, out_sem):
    size = BLOCKS // PIECES
    pieces = [pl.ds(i * size, size) for i in range(PIECES)]
    ins = [
        pltpu.make_async_copy(src.at[at], held.at[at], in_sem.at[i]) for i, at in enumerate(pieces)
    ]
    outs = [
        pltpu.make_async_copy(held.at[at], dst.at[at], out_sem.at[i]) for i, at in enumerate(pieces)
    ]
    for copy in ins:
        copy.start()
    for into, onward in zip(ins, outs):
        into.wait()
        onward.start()
    for copy in outs:
        copy.wait()


def local(cotangent, departure, interp, vertical_inv, regime, bed_rate):
    hbm = pl.BlockSpec(memory_space=pltpu.HBM)
    dma = pltpu.SemaphoreType.DMA
    result = pl.pallas_call(
        kernel,
        out_shape=jax.ShapeDtypeStruct((BLOCKS, LAYERS, COLS), F32),
        in_specs=[hbm] * 5 + [pl.BlockSpec(memory_space=pltpu.SMEM)],
        out_specs=hbm,
        scratch_shapes=[
            pltpu.VMEM((BLOCKS, LAYERS, COLS), F32),
            pltpu.VMEM((STEPS, CELLS * BLOCKS), jnp.int32),
            pltpu.VMEM((STEPS, OWN, COLS, COLS), BF16),
            pltpu.VMEM((CLS, NSET, LAYERS, LAYERS), F32),
            pltpu.VMEM((BLOCKS, COLS), jnp.int32),
            pltpu.VMEM((STEPS, CHUNKS, CLS, ROWS, COLS), BF16),
            pltpu.VMEM((STEPS, CHUNKS, CLS - 1, ROWS, COLS), BF16),
            pltpu.VMEM((STEPS, CHUNKS, CLS - 1, ROWS, COLS), BF16),
            pltpu.VMEM((STEPS, CHUNKS, CLS, ROWS, COLS), BF16),
            pltpu.VMEM((STEPS, CHUNKS, REACH, ROWS, COLS), BF16),
            pltpu.VMEM((STEPS, CHUNKS, REACH, ROWS, COLS), BF16),
            pltpu.VMEM((LAYERS * PITCH, COLS), F32),
            pltpu.VMEM((LAYERS * BLOCKS, COLS), F32),
            pltpu.VMEM((CLS, CHUNK * STEP, COLS), F32),
            pltpu.VMEM((STEPS, BLOCKS, COLS), F32),
            pltpu.VMEM((STEPS, CLS - 1, BLOCKS, COLS), F32),
            pltpu.VMEM((BLOCKS, COLS), F32),
            pltpu.VMEM((NSET * LAYERS, 4 * LAYERS), BF16),
            pltpu.VMEM((STEPS, BLOCKS, BLOCKS), BF16),
            pltpu.VMEM((STEPS, BLOCKS, 2 * BLOCKS), BF16),
            dma((6,)),
            dma((CHUNKS,)),
        ]
        + [dma((STEPS, CLS, CLS - 1))] * 2
        + [dma((STEPS, CHUNKS, CLS - 1))] * 2
        + [dma((STEPS, CHUNKS, 2, CLS - 1))] * 2
        + [dma((STEPS, CHUNKS, 2, REACH))] * 2,
        compiler_params=pltpu.CompilerParams(
            collective_id=0, has_side_effects=True, vmem_limit_bytes=56 * 1024 * 1024
        ),
        cost_estimate=pl.CostEstimate(flops=2_000_000_000, bytes_accessed=6_000_000, transcendentals=0),
    )(cotangent[0], departure, interp, vertical_inv, regime, bed_rate)
    return pl.pallas_call(
        place_result,
        out_shape=jax.ShapeDtypeStruct((BLOCKS, LAYERS, COLS), F32),
        in_specs=[hbm],
        out_specs=hbm,
        scratch_shapes=[pltpu.VMEM((BLOCKS, LAYERS, COLS), F32), dma((PIECES,)), dma((PIECES,))],
        compiler_params=pltpu.CompilerParams(vmem_limit_bytes=56 * 1024 * 1024),
    )(result)[None]


def solution(mesh):
    placed = (
        P("cls", "cells", None, None),
        P(),
        P(None, ("cells", "cls"), None, None),
        P(),
        P("cells", None),
        P(),
    )
    return jax.shard_map(
        local, mesh=mesh, in_specs=placed, out_specs=P("cls", "cells", None, None), check_vma=False
    )
```

```python
import jax
import jax.numpy as jnp
from jax import lax
from jax.experimental import pallas as pl
from jax.experimental.pallas import tpu as pltpu
from jax.sharding import PartitionSpec as P

CELLS = 64
CLS = 4
BLOCKS = 128
OWN = BLOCKS // CLS
LAYERS = 24
COLS = 128
NSET = 4
REACH = 4
CAP = 32
STEPS = 2
CHUNK = 8
CHUNKS = LAYERS // CHUNK
ORDER = (2, 1, 0)
DESTS = (2, 1, 3, 0)
PIECES = 4
ROWS = CHUNK * OWN
STEP = OWN + 8
PITCH = BLOCKS + 8
HALF = ROWS // 2
V_PAIRS = 16
I_PAIRS = 16
MESH = pl.DeviceIdType.MESH
F32 = jnp.float32
BF16 = jnp.bfloat16


def iota(shape, dim):
    return lax.broadcasted_iota(jnp.int32, shape, dim)


def ones_where(mask):
    return jnp.where(mask, F32(1.0), F32(0.0)).astype(BF16)


def nt_dot(a, b, **kw):
    return lax.dot_general(a, b, (((1,), (1,)), ((), ())), preferred_element_type=F32, **kw)


def build_operators(v_ref, lhs, cls):
    eye = jnp.where(iota((LAYERS, LAYERS), 0) == iota((LAYERS, LAYERS), 1), F32(1.0), F32(0.0))
    shape = (LAYERS, 4 * LAYERS)
    col, row = iota(shape, 1), iota(shape, 0)
    place_high = ones_where((col == row) | (col == row + LAYERS))
    place_low = ones_where((col == row + 2 * LAYERS) | (col == row + 3 * LAYERS))
    parts = []
    for r in range(NSET):
        turned = nt_dot(eye, v_ref[cls, r], precision=lax.Precision.HIGHEST)
        high = turned.astype(BF16)
        low = (turned - high.astype(F32)).astype(BF16)
        parts.append(
            jnp.dot(high, place_high, preferred_element_type=F32)
            + jnp.dot(low, place_low, preferred_element_type=F32)
        )
    lhs[...] = jnp.concatenate(parts, axis=0).astype(BF16)


def route(dep, s, q):
    row = dep[s : s + 1, pl.ds(pl.multiple_of(q * BLOCKS, BLOCKS), BLOCKS)]
    off = q - (row >> 7)
    tgt = row & (BLOCKS - 1)
    hot = jnp.where(iota((16, BLOCKS), 0) == off, F32(1.0), F32(0.0))
    tri = ones_where(iota((BLOCKS, BLOCKS), 0) < iota((BLOCKS, BLOCKS), 1))
    before = jnp.dot(hot.astype(BF16), tri, preferred_element_type=F32)
    rank = jnp.sum(before * hot, axis=0, keepdims=True).astype(jnp.int32)
    slot = jnp.where(off > 0, (off - 1) * CAP + rank, -1)
    return off, tgt, slot


def build_tables(dep, gather, total, s, me):
    square = (BLOCKS, BLOCKS)
    off, tgt, slot = route(dep, s, me)
    gather[s] = ones_where(iota(square, 0) == slot)
    total[s, :, :BLOCKS] = ones_where(iota(square, 0) == jnp.where(off == 0, tgt, -1))
    remote = jnp.zeros(square, F32)
    for d in range(1, REACH + 1):
        off, tgt, slot = route(dep, s, lax.rem(me + d, CELLS))
        aims = ones_where(iota(square, 0) == tgt)
        slots = ones_where(iota(square, 0) == jnp.where(off == d, slot, -1))
        remote = remote + nt_dot(aims, slots)
    total[s, :, BLOCKS:] = remote.astype(BF16)


def kernel(
    cot_hbm, dep_hbm, w_hbm, v_hbm, reg_hbm, rate, out,
    cot, dep, w, v_ref, reg, adj, ra, sb, pr, xs, xr, fs, ob, pf, bed_out, bed_in, bot, lhs,
    gather, total, load_sem, out_sem, bed_s, bed_r, a1_s, a1_r, a2_s, a2_r, x_s, x_r,
):
    me = lax.axis_index("cells")
    cls = lax.axis_index("cls")

    split = LAYERS - CHUNK
    arrays = [
        (cot_hbm.at[:, split:, :], cot.at[:, split:, :]),
        (cot_hbm.at[:, :split, :], cot.at[:, :split, :]),
        (v_hbm, v_ref),
        (reg_hbm, reg),
        (dep_hbm, dep),
        (w_hbm, w),
    ]
    loads = [
        pltpu.make_async_copy(src, dst, load_sem.at[i]) for i, (src, dst) in enumerate(arrays)
    ]
    for copy in loads:
        copy.start()

    def over_y(k):
        return (me, lax.rem(cls + k, CLS))

    def along(d):
        return (lax.rem(me + d + CELLS, CELLS), cls)

    barrier = pltpu.get_barrier_semaphore()
    partners = [over_y(k) for k in range(1, CLS)]
    partners += [along(d) for d in range(-REACH, REACH + 1) if d != 0]
    for partner in partners:
        pl.semaphore_signal(barrier, inc=1, device_id=partner, device_id_type=MESH)

    pending = []

    def send(src, dst, ssem, rsem, device):
        copy = pltpu.make_async_remote_copy(
            src_ref=src, dst_ref=dst, send_sem=ssem, recv_sem=rsem,
            device_id=device, device_id_type=MESH,
        )
        copy.start()
        pending.append(copy)
        return copy

    my_rate = rate[cls]

    def own_rows(dest):
        return pl.ds(pl.multiple_of(dest * OWN, OWN), OWN)

    def send_bed(s):
        copies = {}
        for i in DESTS:
            for k in DESTS[:-1]:
                at = own_rows(lax.rem(cls + k + i, CLS))
                copies[i, k] = send(
                    bed_out.at[s, at], bed_in.at[s, k - 1, at],
                    bed_s.at[s, i, k - 1], bed_r.at[s, i, k - 1], over_y(k),
                )
        return copies

    def bottom_of(s, copies, i, dest):
        at = own_rows(dest)
        for k in range(1, CLS):
            copies[i, k].wait_recv()
        return bed_out[s, at] + bed_in[s, 0, at] + bed_in[s, 1, at] + bed_in[s, 2, at]

    def vertical(s, load, dest):
        def operands(b):
            field = jnp.concatenate([load(b), load(b + 1)], axis=1)
            high = field.astype(BF16).astype(F32)
            low = field - high
            return jnp.concatenate([high, low, high, low], axis=0).astype(BF16)

        def pick(b, res):
            r = jnp.concatenate([reg[pl.ds(b, 1), :], reg[pl.ds(b + 1, 1), :]], axis=1)
            picked = res[:LAYERS]
            for i in range(1, NSET):
                picked = jnp.where(r == i, res[i * LAYERS : (i + 1) * LAYERS], picked)
            return picked

        def body(g, carry):
            ns = [g * V_PAIRS + i for i in range(V_PAIRS)]
            bs = [dest * OWN + 2 * n for n in ns]
            rhs = [operands(b) for b in bs]
            res = [jnp.dot(lhs[...], x, preferred_element_type=F32) for x in rhs]
            for n, b, x in zip(ns, bs, res):
                picked = pick(b, x)
                at = pl.ds(pl.multiple_of(n * 16, 16), 16)
                for lc in range(CHUNKS):
                    part = picked[lc * CHUNK : (lc + 1) * CHUNK]
                    both = jnp.concatenate([part[:, :COLS], part[:, COLS:]], axis=0)
                    adj[s, lc, dest, at, :] = both.astype(BF16)
            return carry

        lax.fori_loop(0, OWN // 2 // V_PAIRS, body, 0)

    def interpolate(s, lc):
        def body(g, carry):
            ns = [g * I_PAIRS + i for i in range(I_PAIRS)]
            res = []
            for n in ns:
                at = pl.ds(pl.multiple_of(n * 16, 16), 16)
                tiles = [adj[s, lc, cls, at, :]] + [ra[s, lc, k, at, :] for k in range(CLS - 1)]
                weights = jnp.concatenate([w[s, 2 * n], w[s, 2 * n + 1]], axis=1)
                res.append(
                    jnp.dot(jnp.concatenate(tiles, axis=0), weights, preferred_element_type=F32)
                )
            for n, x in zip(ns, res):
                for k in range(CLS):
                    pf[k, pl.ds(2 * n, CHUNK, stride=STEP), :] = x[k * 16 : k * 16 + 8, :COLS]
                    pf[k, pl.ds(2 * n + 1, CHUNK, stride=STEP), :] = x[k * 16 + 8 : k * 16 + 16, COLS:]
            return carry

        lax.fori_loop(0, OWN // 2 // I_PAIRS, body, 0)
        for i in range(CHUNK):
            at, packed = pl.ds(i * STEP, OWN), pl.ds(i * OWN, OWN)
            for k in range(1, CLS):
                sb[s, lc, k - 1, packed, :] = pf[k, at, :].astype(BF16)
            pr[s, lc, cls, packed, :] = pf[0, at, :].astype(BF16)

    def plane_of(s, lc, at):
        return jnp.concatenate([pr[s, lc, y, at, :] for y in range(CLS)], axis=0)

    def pairs(lc, h):
        for n in range(CHUNK // 4):
            at = h * CHUNK // 2 + 2 * n
            yield [pl.ds((at + i) * OWN, OWN) for i in range(2)], lc * CHUNK + at

    def pack(s, lc, h):
        for ats, _ in pairs(lc, h):
            rhs = jnp.concatenate([plane_of(s, lc, at) for at in ats], axis=1)
            res = jnp.dot(gather[s], rhs, preferred_element_type=F32).astype(BF16)
            for d in range(REACH):
                for i, at in enumerate(ats):
                    xs[s, lc, d, at, :] = res[d * CAP : (d + 1) * CAP, i * COLS : (i + 1) * COLS]

    def accumulate(s, lc, h, dst, place):
        for ats, layer in pairs(lc, h):
            cols = [
                jnp.concatenate(
                    [plane_of(s, lc, at)] + [xr[s, lc, d, at, :] for d in range(REACH)], axis=0
                )
                for at in ats
            ]
            res = jnp.dot(total[s], jnp.concatenate(cols, axis=1), preferred_element_type=F32)
            for i in range(2):
                dst[place(layer + i), :] = res[:, i * COLS : (i + 1) * COLS]

    first = STEPS - 1
    tail = (LAYERS - 1) * PITCH
    loads[0].wait()
    bed_out[first] = my_rate * cot[:, LAYERS - 1, :]
    pl.semaphore_wait(barrier, len(partners))
    beds = send_bed(first)
    for copy in loads[1:]:
        copy.wait()
    build_operators(v_ref, lhs, cls)
    for s in range(STEPS):
        build_tables(dep, gather, total, s, me)

    stores = []
    for s in range(STEPS - 1, -1, -1):
        if s == first:
            last = iota((LAYERS, COLS), 0) == LAYERS - 1

            def add_bottom(i, dest):
                bot[own_rows(dest)] = bottom_of(s, beds, i, dest)

            def load(b):
                return cot[b] + jnp.where(last, bot[pl.ds(b, 1), :], F32(0.0))
        else:

            def add_bottom(i, dest):
                at = pl.ds(pl.multiple_of(tail + dest * OWN, 8), OWN)
                fs[at, :] = fs[at, :] + bottom_of(s, beds, i, dest)

            def load(b):
                return fs[pl.ds(b, LAYERS, stride=PITCH), :]

        a1, a2, x = {}, {}, {}

        def send_adjoint(lc, k):
            a1[lc, k] = send(
                adj.at[s, lc, lax.rem(cls + k, CLS)], ra.at[s, lc, k - 1],
                a1_s.at[s, lc, k - 1], a1_r.at[s, lc, k - 1], over_y(k),
            )

        def exchange(lc):
            for k in range(1, CLS):
                a1[lc, k].wait_recv()
            interpolate(s, lc)

        def rows(h):
            return pl.ds(h * HALF, HALF)

        def send_back(lc, h):
            for k in (2, 1, 3):
                a2[lc, h, k] = send(
                    sb.at[s, lc, k - 1, rows(h)], pr.at[s, lc, cls, rows(h)],
                    a2_s.at[s, lc, h, k - 1], a2_r.at[s, lc, h, k - 1], over_y(CLS - k),
                )

        def depart(lc, h):
            for k in range(1, CLS):
                a2[lc, h, k].wait_recv()
            pack(s, lc, h)
            for d in range(REACH, 0, -1):
                x[lc, h, d] = send(
                    xs.at[s, lc, d - 1, rows(h)], xr.at[s, lc, d - 1, rows(h)],
                    x_s.at[s, lc, h, d - 1], x_r.at[s, lc, h, d - 1], along(-d),
                )

        def arrive(lc, h):
            for d in range(1, REACH + 1):
                x[lc, h, d].wait_recv()
            if s > 0:
                accumulate(s, lc, h, fs, lambda layer: pl.ds(layer * PITCH, BLOCKS))
                return
            accumulate(s, lc, h, ob, lambda layer: pl.ds(layer, BLOCKS, stride=LAYERS))
            if h == 1:
                at = pl.ds(lc * CHUNK, CHUNK)
                copy = pltpu.make_async_copy(
                    ob.reshape(BLOCKS, LAYERS, COLS).at[:, at, :], out.at[:, at, :], out_sem.at[lc]
                )
                copy.start()
                stores.append(copy)

        c0, c1, c2 = ORDER
        for i in DESTS:
            dest = lax.rem(cls + i, CLS)
            add_bottom(i, dest)
            vertical(s, load, dest)
            if i:
                send_adjoint(c0, i)
        for k in DESTS[:-1]:
            send_adjoint(c1, k)
        exchange(c0)
        send_back(c0, 0)
        send_back(c0, 1)
        exchange(c1)
        send_back(c1, 0)
        for k in DESTS[:-1]:
            send_adjoint(c2, k)
        send_back(c1, 1)
        depart(c0, 0)
        depart(c0, 1)
        depart(c1, 0)
        exchange(c2)
        send_back(c2, 0)
        send_back(c2, 1)
        depart(c1, 1)
        depart(c2, 0)
        arrive(c0, 0)
        arrive(c0, 1)
        if s > 0:
            bed_out[s - 1] = my_rate * fs[pl.ds(tail, BLOCKS), :]
            beds = send_bed(s - 1)
        depart(c2, 1)
        arrive(c1, 0)
        arrive(c1, 1)
        arrive(c2, 0)
        arrive(c2, 1)

    for copy in pending:
        copy.wait_send()
    for copy in stores:
        copy.wait()


def place_result(src, dst, held, in_sem, out_sem):
    size = BLOCKS // PIECES
    pieces = [pl.ds(i * size, size) for i in range(PIECES)]
    ins = [
        pltpu.make_async_copy(src.at[at], held.at[at], in_sem.at[i]) for i, at in enumerate(pieces)
    ]
    outs = [
        pltpu.make_async_copy(held.at[at], dst.at[at], out_sem.at[i]) for i, at in enumerate(pieces)
    ]
    for copy in ins:
        copy.start()
    for into, onward in zip(ins, outs):
        into.wait()
        onward.start()
    for copy in outs:
        copy.wait()


def local(cotangent, departure, interp, vertical_inv, regime, bed_rate):
    hbm = pl.BlockSpec(memory_space=pltpu.HBM)
    dma = pltpu.SemaphoreType.DMA
    result = pl.pallas_call(
        kernel,
        out_shape=jax.ShapeDtypeStruct((BLOCKS, LAYERS, COLS), F32),
        in_specs=[hbm] * 5 + [pl.BlockSpec(memory_space=pltpu.SMEM)],
        out_specs=hbm,
        scratch_shapes=[
            pltpu.VMEM((BLOCKS, LAYERS, COLS), F32),
            pltpu.VMEM((STEPS, CELLS * BLOCKS), jnp.int32),
            pltpu.VMEM((STEPS, OWN, COLS, COLS), BF16),
            pltpu.VMEM((CLS, NSET, LAYERS, LAYERS), F32),
            pltpu.VMEM((BLOCKS, COLS), jnp.int32),
            pltpu.VMEM((STEPS, CHUNKS, CLS, ROWS, COLS), BF16),
            pltpu.VMEM((STEPS, CHUNKS, CLS - 1, ROWS, COLS), BF16),
            pltpu.VMEM((STEPS, CHUNKS, CLS - 1, ROWS, COLS), BF16),
            pltpu.VMEM((STEPS, CHUNKS, CLS, ROWS, COLS), BF16),
            pltpu.VMEM((STEPS, CHUNKS, REACH, ROWS, COLS), BF16),
            pltpu.VMEM((STEPS, CHUNKS, REACH, ROWS, COLS), BF16),
            pltpu.VMEM((LAYERS * PITCH, COLS), F32),
            pltpu.VMEM((LAYERS * BLOCKS, COLS), F32),
            pltpu.VMEM((CLS, CHUNK * STEP, COLS), F32),
            pltpu.VMEM((STEPS, BLOCKS, COLS), F32),
            pltpu.VMEM((STEPS, CLS - 1, BLOCKS, COLS), F32),
            pltpu.VMEM((BLOCKS, COLS), F32),
            pltpu.VMEM((NSET * LAYERS, 4 * LAYERS), BF16),
            pltpu.VMEM((STEPS, BLOCKS, BLOCKS), BF16),
            pltpu.VMEM((STEPS, BLOCKS, 2 * BLOCKS), BF16),
            dma((6,)),
            dma((CHUNKS,)),
        ]
        + [dma((STEPS, CLS, CLS - 1))] * 2
        + [dma((STEPS, CHUNKS, CLS - 1))] * 2
        + [dma((STEPS, CHUNKS, 2, CLS - 1))] * 2
        + [dma((STEPS, CHUNKS, 2, REACH))] * 2,
        compiler_params=pltpu.CompilerParams(
            collective_id=0, has_side_effects=True, vmem_limit_bytes=56 * 1024 * 1024
        ),
        cost_estimate=pl.CostEstimate(flops=2_000_000_000, bytes_accessed=6_000_000, transcendentals=0),
    )(cotangent[0], departure, interp, vertical_inv, regime, bed_rate)
    return pl.pallas_call(
        place_result,
        out_shape=jax.ShapeDtypeStruct((BLOCKS, LAYERS, COLS), F32),
        in_specs=[hbm],
        out_specs=hbm,
        scratch_shapes=[pltpu.VMEM((BLOCKS, LAYERS, COLS), F32), dma((PIECES,)), dma((PIECES,))],
        compiler_params=pltpu.CompilerParams(vmem_limit_bytes=56 * 1024 * 1024),
    )(result)[None]


def solution(mesh):
    placed = (
        P("cls", "cells", None, None),
        P(),
        P(None, ("cells", "cls"), None, None),
        P(),
        P("cells", None),
        P(),
    )
    return jax.shard_map(
        local, mesh=mesh, in_specs=placed, out_specs=P("cls", "cells", None, None), check_vma=False
    )
```
